32 devices in a mesh: grp: 2 (over y), node: 4 (over z), rank: 4 (over x, core).
Axes of the slice: x: 2, y: 2, z: 4, core: 2. Of those that a mesh axis runs over, the one named last changes fastest.
Arguments:
- tokens: bfloat16 [1024, 2048], P(('grp', 'node', 'rank')), parts along dimension 0, may hold values from -6 to 6
- expert_ids: int32 [1024, 10], P(('grp', 'node', 'rank')), parts along dimension 0, may hold values from 0 to 31, all different within a row; in each aligned block of 32 rows (0 to 31, 32 to 63, ...) at most 15 rows name the same one
- combine_weights: int32 [1024, 10], P(('grp', 'node', 'rank')), parts along dimension 0, may hold values from 16384 to 65535
- slot_plan: int32 [32], replicated, may hold values from 0 to 31, each once
- w_gate: bfloat16 [32, 2048, 512], P(('node', 'rank')), may hold values from -0.125 to 0.125
- w_up: bfloat16 [32, 2048, 512], P(('node', 'rank')), may hold values from -0.125 to 0.125
- w_down: bfloat16 [32, 512, 2048], P(('node', 'rank')), may hold values from -0.25 to 0.25
Outputs:
- mixed: bfloat16 [1024, 2048], P(('grp', 'node', 'rank')), parts along dimension 0
The draws below stay inside these ranges and needn't reach their ends.
There are 2 independent parts, one for each index of `grp`. The reference program is written for one: setup_inputs(seed, part) draws one part's arguments, and reference() takes and returns one part's arrays. A program takes and returns all parts, laid end to end along the dimension named above; an argument that names none is the same for every part. Nothing has to cross between parts.
Inputs may be any that keep to these rules, and one draw needn't show every extreme that they name: `expert_ids`: each row names 10 different experts; among the rows of one device no expert is named more than 15 times, and in every draw some expert reaches 15. `slot_plan`: each slot once.
All inputs are finite; a program needn't handle non-finite values.
Results may differ from the reference program's by a relative error of at most 0.0058.
Values may be sent and summed in bfloat16 or wider, within the bound.
No kernel may reach another device: no remote copies, remote signals or barrier semaphores. Data moves between devices by JAX's collectives and lax.ppermute only.
A program may use at most 64 MiB of HBM per device.

```python
import math
import jax
import jax.numpy as jnp
import numpy as np
from jax import lax

D = 2048
FF = 512
TOP = 10
TOK_DEV = 32
EXPERTS = 32
TOKENS = 512
CAP = 15
ROWS = 240


def touch_ends(drawn, stream_key, smallest, high):
    longest = drawn.shape.index(max(drawn.shape))
    spots = []
    for shift in (0, 1):
        where = [jax.random.randint(jax.random.fold_in(stream_key, axis), (), 0, length) for axis, length in enumerate(drawn.shape)]
        where[longest] = (where[longest] + shift) % drawn.shape[longest]
        spots.append(tuple(where))
    return drawn.at[spots[0]].set(smallest).at[spots[1]].set(high)


def levels(key, extent, shards, smallest, high):
    factor_of, own = 1.0, jax.random.fold_in(key, 6)
    for dim, parts in shards:
        heights = jnp.exp(jax.random.uniform(jax.random.fold_in(own, dim), (parts,), jnp.float32, smallest / len(shards), high / len(shards)))
        factor_of = factor_of * jnp.repeat(heights, extent[dim] // parts).reshape([-1 if axis == dim else 1 for axis in range(len(extent))])
    return factor_of


def routed_block(own_key, own, number, rows, count, top, bound, skew):
    ranking = jax.random.permutation(own_key, count)
    heavy_load, ordinary = shares(count, rows * top, bound, skew, True), shares(count, rows * top, bound, skew, False)
    places = jnp.arange(count)

    def named(tallies, rotation):
        used = int((tallies > 0).sum())
        fixed = max(1, used // 4)
        shifted = fixed + (places - fixed + rotation * (used - fixed)) % max(1, count - fixed)
        return jnp.zeros((count,), jnp.int32).at[ranking[jnp.where(places < fixed, places, shifted)]].set(jnp.asarray(tallies, jnp.int32))

    tallies = jnp.where(number % 4 == 0, named(heavy_load, number // 4), named(ordinary, number - number // 4 - 1))
    mixed = jax.random.permutation(jax.random.fold_in(own, 3), count)
    donor, receiver = mixed[0:count // 2 * 2:2], mixed[1:count // 2 * 2:2]
    slack = jnp.minimum(tallies[donor] - 1, bound - tallies[receiver]) // 2
    slack = jnp.where((donor == ranking[0]) | (receiver == ranking[0]) | (tallies[receiver] == 0), 0, jnp.maximum(slack, 0))
    shifted = jax.random.randint(jax.random.fold_in(own, 4), (count // 2,), 0, 1 << 20) % (slack + 1)
    tallies = tallies.at[donor].add(-shifted).at[receiver].add(shifted)
    labels = jnp.searchsorted(jnp.cumsum(tallies), jnp.arange(rows * top), side="right").astype(jnp.int32)
    grid = labels.reshape(top, rows).T
    grid = grid[jax.random.permutation(jax.random.fold_in(own, 1), rows)]
    rotation = jax.random.randint(jax.random.fold_in(own, 2), (rows, 1), 0, top)
    return jnp.take_along_axis(grid, (jnp.arange(top)[None, :] + rotation) % top, axis=1)


def shares(count, total, most, slope, full):
    weights = [(1 << 20) // math.isqrt(standing ** slope) + 1 for standing in range(1, count + 1)]
    largest = most if full else min(most, max(-(-total // count), total * weights[0] // sum(weights)))
    least = 1 if total - largest >= count - 1 else 0
    counts, rest = [largest] + [least] * (count - 1), total - largest - least * (count - 1)
    while rest > 0:
        movable = [i for i in range(1, count) if counts[i] < largest] or [i for i in range(1, count) if counts[i] < most]
        pool, remaining = sum([weights[i] for i in movable]), rest
        for i in movable:
            more = min(most - counts[i], max(1, remaining * weights[i] // pool), rest)
            counts[i] = counts[i] + more
            rest = rest - more
    return np.array(counts)


def normal_values(stream_key, extent, width, limit, split=(), kind=jnp.bfloat16):
    values = width * jax.random.normal(stream_key, extent, jnp.float32)
    if split:
        values = values * levels(stream_key, extent, split, -0.22, 0.18)
    return jnp.clip(values, -limit, limit).astype(kind)


def setup_inputs(seed: int = 0, part: int = 0) -> dict:
    streams_of = jax.random.split(jax.random.key(seed), 8)
    part_splits = jax.random.split(jax.random.fold_in(streams_of[7], part), 8)
    tokens = normal_values(part_splits[0], (TOKENS, D), 1.0, 6.0, ((0, 16),))
    expert_ids_keys = jax.random.split(jax.random.fold_in(part_splits[1], 1), TOKENS // TOK_DEV)
    expert_ids_turns = jax.random.permutation(jax.random.fold_in(part_splits[1], 3), TOKENS // TOK_DEV)
    expert_ids = jax.vmap(lambda own, number: routed_block(jax.random.fold_in(part_splits[1], 2), own, number, TOK_DEV, EXPERTS, TOP, CAP, 2))(expert_ids_keys, expert_ids_turns).reshape((TOKENS, TOP))
    combine_weights = touch_ends(jax.random.randint(part_splits[2], (TOKENS, TOP), 16384, 65536), jax.random.fold_in(part_splits[2], 1), 16384, 65535).astype(jnp.int32)
    slot_plan = jax.random.permutation(streams_of[3], EXPERTS).astype(jnp.int32)
    w_gate = normal_values(streams_of[4], (EXPERTS, D, FF), D ** -0.5, 0.125, ((0, 16),))
    w_up = normal_values(streams_of[5], (EXPERTS, D, FF), D ** -0.5, 0.125, ((0, 16),))
    w_down = normal_values(streams_of[6], (EXPERTS, FF, D), FF ** -0.5, 0.25, ((0, 16),))
    return dict(tokens=tokens, expert_ids=expert_ids, combine_weights=combine_weights, slot_plan=slot_plan, w_gate=w_gate, w_up=w_up, w_down=w_down)


def reference(tokens, expert_ids, combine_weights, slot_plan, w_gate, w_up, w_down):
    flat_ids = expert_ids.reshape(-1)
    flat_weights = combine_weights.reshape(-1).astype(jnp.float32) / 65536.0
    lanes = jnp.arange(ROWS, dtype=jnp.int32)

    def one_expert(total, expert):
        slot = slot_plan[expert]
        chosen = flat_ids == expert
        count = jnp.sum(chosen.astype(jnp.int32))
        picked = jnp.nonzero(chosen, size=ROWS, fill_value=0)[0].astype(jnp.int32)
        token_rows = (picked // TOP).astype(jnp.int32)
        rows = tokens[token_rows]
        gate = jnp.dot(rows, w_gate[slot], preferred_element_type=jnp.float32)
        up = jnp.dot(rows, w_up[slot], preferred_element_type=jnp.float32)
        hidden = (jax.nn.silu(gate) * up).astype(jnp.bfloat16)
        result = jnp.dot(hidden, w_down[slot], preferred_element_type=jnp.float32).astype(jnp.bfloat16)
        scale = jnp.where(lanes < count, flat_weights[picked], 0.0).astype(jnp.float32)
        total = total.at[token_rows].add(result.astype(jnp.float32) * scale[:, None])
        return total, None

    start = jnp.zeros((TOKENS, D), jnp.float32)
    total, _ = lax.scan(one_expert, start, jnp.arange(EXPERTS, dtype=jnp.int32))
    return total.astype(jnp.bfloat16)
```

```python
import functools

import jax
import jax.numpy as jnp
from jax import lax
from jax.experimental import pallas as pl
from jax.experimental.pallas import tpu as pltpu
from jax.sharding import PartitionSpec as P

LANES = 128
VMEM = pl.BlockSpec(memory_space=pltpu.VMEM)
SMEM = pl.BlockSpec(memory_space=pltpu.SMEM)


def capacity_of(tok_rows, top, slots):
    return max(2, (3 * tok_rows * top + 2 * slots - 1) // (2 * slots))


def routed(tokens, expert_ids, combine_weights, slot_plan, w_gate, w_up, w_down):
    n_dev = lax.axis_size("node") * lax.axis_size("rank")
    exp_dev = w_gate.shape[0]
    slots = n_dev * exp_dev
    tok_rows, top = expert_ids.shape
    width = tokens.shape[1]
    capacity = capacity_of(tok_rows, top, slots)
    flat_ids = expert_ids.reshape(-1)
    onehot = (flat_ids[:, None] == jnp.arange(slots, dtype=jnp.int32)[None, :]).astype(jnp.int32)
    slot_of = jnp.sum(onehot * slot_plan[None, :], axis=1)
    earlier = jnp.cumsum(onehot, axis=0) - onehot
    position = jnp.sum(earlier * onehot, axis=1)
    target = slot_of * capacity + position
    repeated = jnp.repeat(tokens, top, axis=0)
    outgoing = jnp.zeros((slots * capacity, width), jnp.bfloat16).at[target].set(repeated)
    flat_out = outgoing.reshape(n_dev, exp_dev * capacity, width)
    arrived = lax.all_to_all(flat_out, ("node", "rank"), split_axis=0, concat_axis=0, tiled=True)
    arrived = arrived.reshape(n_dev, exp_dev, capacity, width)
    gate = jnp.einsum("secd,edf->secf", arrived, w_gate, preferred_element_type=jnp.float32)
    up = jnp.einsum("secd,edf->secf", arrived, w_up, preferred_element_type=jnp.float32)
    hidden = (jax.nn.silu(gate) * up).astype(jnp.bfloat16)
    result = jnp.einsum("secf,efd->secd", hidden, w_down, preferred_element_type=jnp.float32).astype(jnp.bfloat16)
    flat_back = result.reshape(n_dev, exp_dev * capacity, width)
    returned = lax.all_to_all(flat_back, ("node", "rank"), split_axis=0, concat_axis=0, tiled=True)
    returned = returned.reshape(slots * capacity, width)
    picked = returned[target].reshape(tok_rows, top, width)
    scales = combine_weights.astype(jnp.float32) / 65536.0
    mixed = jnp.sum(picked.astype(jnp.float32) * scales[:, :, None], axis=1)
    return mixed.astype(jnp.bfloat16)


def ffn_kernel(mine_ref, *refs, blocks, top):
    ins, (wg_ref, wu_ref, wd_ref, near_ref, far_ref, rows) = refs[:blocks], refs[blocks:]
    width = near_ref.shape[1]
    step = ins[0].shape[0]
    for i, ref in enumerate(ins):
        rows[pl.ds(i * step, step), :] = ref[...]
    x = rows[:, :width]
    meta = rows[:, width:].astype(jnp.float32)
    ids, weight = meta[:, :top], (meta[:, top : 2 * top] * 256.0 + meta[:, 2 * top : 3 * top]) * (1.0 / 65536.0)
    total = None
    for e in range(wg_ref.shape[0]):
        scale = jnp.sum(jnp.where(ids == mine_ref[e].astype(jnp.float32), weight, 0.0), axis=1, keepdims=True)
        gate = jnp.dot(x, wg_ref[e], preferred_element_type=jnp.float32)
        up = jnp.dot(x, wu_ref[e], preferred_element_type=jnp.float32)
        hidden = (gate / (1.0 + jnp.exp(-gate)) * up).astype(jnp.bfloat16)
        part = jnp.dot(hidden, wd_ref[e], preferred_element_type=jnp.float32) * scale
        total = part if total is None else total + part
    half = near_ref.shape[0]
    near_ref[...] = total[:half]
    far_ref[...] = total[half:].astype(far_ref.dtype)


def ffn(mine, blocks, w_gate, w_up, w_down, top):
    width = w_gate.shape[1]
    rows = sum(b.shape[0] for b in blocks)
    return pl.pallas_call(
        functools.partial(ffn_kernel, blocks=len(blocks), top=top),
        out_shape=(
            jax.ShapeDtypeStruct((rows // 2, width), jnp.float32),
            jax.ShapeDtypeStruct((rows // 2, width), jnp.bfloat16),
        ),
        in_specs=[SMEM] + [VMEM] * (len(blocks) + 3),
        out_specs=(VMEM, VMEM),
        scratch_shapes=[pltpu.VMEM((rows, blocks[0].shape[1]), jnp.bfloat16)],
        compiler_params=pltpu.CompilerParams(vmem_limit_bytes=24 << 20),
        name=f"ffn_{rows}",
    )(mine, *blocks, w_gate, w_up, w_down)


def join_kernel(near_ref, other_ref, *out_refs):
    step = out_refs[0].shape[0]
    for i, ref in enumerate(out_refs):
        part = near_ref[pl.ds(i * step, step), :] + other_ref[pl.ds(i * step, step), :].astype(jnp.float32)
        ref[...] = part.astype(ref.dtype)


def join(near, other, types):
    step = near.shape[0] // len(types)
    return pl.pallas_call(
        join_kernel,
        out_shape=tuple(jax.ShapeDtypeStruct((step, near.shape[1]), t) for t in types),
        in_specs=[VMEM, VMEM],
        out_specs=(VMEM,) * len(types),
        compiler_params=pltpu.CompilerParams(vmem_limit_bytes=16 << 20),
        name="join",
    )(near, other)


def total_kernel(*refs):
    total = refs[0][...].astype(jnp.float32)
    for ref in refs[1:-1]:
        total += ref[...].astype(jnp.float32)
    refs[-1][...] = total.astype(refs[-1].dtype)


def add_up(parts, dtype):
    return pl.pallas_call(
        total_kernel,
        out_shape=jax.ShapeDtypeStruct(parts[0].shape, dtype),
        in_specs=[VMEM] * len(parts),
        out_specs=VMEM,
        compiler_params=pltpu.CompilerParams(vmem_limit_bytes=16 << 20),
        name="total",
    )(*parts)


def dense(tokens, expert_ids, combine_weights, slot_plan, w_gate, w_up, w_down, cores):
    n_node, n_rank = lax.axis_size("node"), lax.axis_size("rank")
    n_x = n_rank // cores
    exp_dev, width = w_gate.shape[:2]
    slots = n_node * n_rank * exp_dev
    top = expert_ids.shape[1]

    def along_z(t, dz):
        return lax.ppermute(t, "node", [(i, i ^ dz) for i in range(n_node)])

    def along_x(t, dx):
        return lax.ppermute(t, "rank", [(i, i ^ (dx * cores)) for i in range(n_rank)])

    def to_chip(t, dz, dx):
        step = dz * n_rank + dx * cores
        return lax.ppermute(t, ("node", "rank"), [(i, i ^ step) for i in range(n_node * n_rank)])

    def swap(t):
        return lax.ppermute(t, "rank", [(i, i ^ 1) for i in range(n_rank)])

    device = lax.axis_index("node") * n_rank + lax.axis_index("rank")
    my_slots = device * exp_dev + jnp.arange(exp_dev, dtype=jnp.int32)
    plan_hit = slot_plan[None, :] == my_slots[:, None]
    mine = jnp.sum(jnp.where(plan_hit, jnp.arange(slots, dtype=jnp.int32)[None, :], 0), axis=1)

    pad = LANES - 3 * top
    meta = jnp.concatenate([expert_ids, combine_weights // 256, combine_weights % 256], axis=1)
    own = jnp.concatenate([tokens, jnp.pad(meta, ((0, 0), (0, pad))).astype(jnp.bfloat16)], axis=1)

    chips = [(dz, dx) for dz in range(n_node) for dx in range(n_x)]
    near = {(0, 0): own}
    for dz in range(1, n_node):
        near[dz, 0] = along_z(own, dz)
    for dz in range(n_node):
        for dx in range(1, n_x):
            near[dz, dx] = along_x(near[dz, 0], dx)
    far = {c: swap(near[c]) for c in chips}

    passes = [chips]
    sums = {}
    for group in passes:
        keep, give = ffn(mine, [near[c] for c in group] + [far[c] for c in group], w_gate, w_up, w_down, top)
        types = [jnp.float32 if c == (0, 0) else jnp.bfloat16 for c in group]
        for c, part in zip(group, join(keep, swap(give), types), strict=True):
            sums[c] = part
    parts = [sums[0, 0]] + [to_chip(sums[c], *c) for c in chips if c != (0, 0)]
    return add_up(parts, tokens.dtype)


def power_of_two(n):
    return n & (n - 1) == 0


def local(tokens, expert_ids, combine_weights, slot_plan, w_gate, w_up, w_down):
    n_node, n_rank = lax.axis_size("node"), lax.axis_size("rank")
    tok_rows, top = expert_ids.shape
    exp_dev = w_gate.shape[0]
    slots = n_node * n_rank * exp_dev
    args = (tokens, expert_ids, combine_weights, slot_plan, w_gate, w_up, w_down)
    sent = exp_dev * capacity_of(tok_rows, top, slots)
    fits = 3 * top <= LANES and slots <= 256 and power_of_two(n_node) and power_of_two(n_rank) and n_rank > 1
    if fits and 2 * sent > tok_rows:
        return dense(*args, cores=2)
    return routed(*args)


def solution(mesh):
    in_specs = (
        P(("grp", "node", "rank"), None),
        P(("grp", "node", "rank"), None),
        P(("grp", "node", "rank"), None),
        P(),
        P(("node", "rank"), None, None),
        P(("node", "rank"), None, None),
        P(("node", "rank"), None, None),
    )
    out_specs = P(("grp", "node", "rank"), None)
    return jax.shard_map(local, mesh=mesh, in_specs=in_specs, out_specs=out_specs, check_vma=False)
```

```python
import functools

import jax
import jax.numpy as jnp
from jax import lax
from jax.experimental import pallas as pl
from jax.experimental.pallas import tpu as pltpu
from jax.sharding import PartitionSpec as P

LANES = 128
VMEM = pl.BlockSpec(memory_space=pltpu.VMEM)
IN_HBM = pl.BlockSpec(memory_space=pltpu.HBM)


def keep_in_hbm(x):
    return pltpu.with_memory_space_constraint(x, pltpu.HBM)


def capacity_of(tok_rows, top, slots):
    return max(2, (3 * tok_rows * top + 2 * slots - 1) // (2 * slots))


def routed(tokens, expert_ids, combine_weights, slot_plan, w_gate, w_up, w_down):
    n_dev = lax.axis_size("node") * lax.axis_size("rank")
    exp_dev = w_gate.shape[0]
    slots = n_dev * exp_dev
    tok_rows, top = expert_ids.shape
    width = tokens.shape[1]
    capacity = capacity_of(tok_rows, top, slots)
    flat_ids = expert_ids.reshape(-1)
    onehot = (flat_ids[:, None] == jnp.arange(slots, dtype=jnp.int32)[None, :]).astype(jnp.int32)
    slot_of = jnp.sum(onehot * slot_plan[None, :], axis=1)
    earlier = jnp.cumsum(onehot, axis=0) - onehot
    position = jnp.sum(earlier * onehot, axis=1)
    target = slot_of * capacity + position
    repeated = jnp.repeat(tokens, top, axis=0)
    outgoing = jnp.zeros((slots * capacity, width), jnp.bfloat16).at[target].set(repeated)
    flat_out = outgoing.reshape(n_dev, exp_dev * capacity, width)
    arrived = lax.all_to_all(flat_out, ("node", "rank"), split_axis=0, concat_axis=0, tiled=True)
    arrived = arrived.reshape(n_dev, exp_dev, capacity, width)
    gate = jnp.einsum("secd,edf->secf", arrived, w_gate, preferred_element_type=jnp.float32)
    up = jnp.einsum("secd,edf->secf", arrived, w_up, preferred_element_type=jnp.float32)
    hidden = (jax.nn.silu(gate) * up).astype(jnp.bfloat16)
    result = jnp.einsum("secf,efd->secd", hidden, w_down, preferred_element_type=jnp.float32).astype(jnp.bfloat16)
    flat_back = result.reshape(n_dev, exp_dev * capacity, width)
    returned = lax.all_to_all(flat_back, ("node", "rank"), split_axis=0, concat_axis=0, tiled=True)
    returned = returned.reshape(slots * capacity, width)
    picked = returned[target].reshape(tok_rows, top, width)
    scales = combine_weights.astype(jnp.float32) / 65536.0
    mixed = jnp.sum(picked.astype(jnp.float32) * scales[:, :, None], axis=1)
    return mixed.astype(jnp.bfloat16)


def rounded(n):
    return -(-n // 8) * 8


def prepare_kernel(tokens_in, ids_in, weights_in, plan_in, rows_ref, mine_ref, ids, weights, meta, plan, sems, *, exp_dev, n_rank):
    width, top = tokens_in.shape[1], ids.shape[0]
    moves = ((tokens_in, rows_ref.at[:, :width]), (ids_in, ids), (weights_in, weights), (plan_in, plan))
    copies = [pltpu.make_async_copy(a, b, sems.at[i]) for i, (a, b) in enumerate(moves)]
    for copy in copies:
        copy.start()
    device = lax.axis_index("node") * n_rank + lax.axis_index("rank")
    copies[3].wait()
    found = [jnp.int32(0)] * exp_dev
    for expert in range(plan.shape[0]):
        slot = plan[expert]
        found = [jnp.where(slot == device * exp_dev + j, expert, f) for j, f in enumerate(found)]
    lane = lax.broadcasted_iota(jnp.int32, mine_ref.shape, 1)
    mine = jnp.zeros(mine_ref.shape, jnp.int32)
    for j, f in enumerate(found):
        mine = jnp.where(lane == j, f, mine)
    mine_ref[...] = mine.astype(jnp.float32)
    copies[1].wait()
    copies[2].wait()
    w = weights[...]
    meta[...] = jnp.zeros(meta.shape, jnp.float32)
    for i, part in enumerate((ids[...], w // 256, w % 256)):
        meta[pl.ds(i * rounded(top), top), :] = part.astype(jnp.float32)
    rows_ref[:, width:] = meta[...].T.astype(rows_ref.dtype)
    copies[0].wait()


def prepare(tokens, expert_ids, combine_weights, slot_plan, exp_dev, n_rank):
    tok_rows, width = tokens.shape
    args = (tokens, expert_ids.T, combine_weights.T, slot_plan)
    return pl.pallas_call(
        functools.partial(prepare_kernel, exp_dev=exp_dev, n_rank=n_rank),
        out_shape=(
            jax.ShapeDtypeStruct((tok_rows, width + LANES), jnp.bfloat16),
            jax.ShapeDtypeStruct((8, LANES), jnp.float32),
        ),
        in_specs=[IN_HBM] * 4,
        out_specs=(VMEM, VMEM),
        scratch_shapes=[
            pltpu.VMEM(args[1].shape, jnp.int32),
            pltpu.VMEM(args[2].shape, jnp.int32),
            pltpu.VMEM((LANES, tok_rows), jnp.float32),
            pltpu.SMEM(slot_plan.shape, jnp.int32),
            pltpu.SemaphoreType.DMA((4,)),
        ],
        compiler_params=pltpu.CompilerParams(vmem_limit_bytes=8 << 20),
        name="prepare",
    )(*map(keep_in_hbm, args))


def experts(x, meta, mine_ref, wg_ref, wu_ref, wd_ref, top, ready=lambda e, i: None):
    gap = rounded(top)
    ids, high, low = (meta[:, i * gap : i * gap + top] for i in range(3))
    weight = (high * 256.0 + low) * (1.0 / 65536.0)
    total = None
    for e in range(wg_ref.shape[0]):
        scale = jnp.sum(jnp.where(ids == mine_ref[0:1, e : e + 1], weight, 0.0), axis=1, keepdims=True)
        ready(e, 0)
        gate = jnp.dot(x, wg_ref[e], preferred_element_type=jnp.float32)
        ready(e, 1)
        up = jnp.dot(x, wu_ref[e], preferred_element_type=jnp.float32)
        hidden = (gate / (1.0 + jnp.exp(-gate)) * up).astype(jnp.bfloat16)
        ready(e, 2)
        part = jnp.dot(hidden, wd_ref[e], preferred_element_type=jnp.float32) * scale
        total = part if total is None else total + part
    return total


def gather_rows(ins, rows, width):
    step = ins[0].shape[0]
    for i, ref in enumerate(ins):
        rows[pl.ds(i * step, step), :] = ref[...]
    return rows[:, :width], rows[:, width:].astype(jnp.float32)


def ffn_kernel(mine_ref, *refs, blocks, top):
    ins, (wg_ref, wu_ref, wd_ref, near_ref, far_ref, rows) = refs[:blocks], refs[blocks:]
    x, meta = gather_rows(ins, rows, near_ref.shape[1])
    total = experts(x, meta, mine_ref, wg_ref, wu_ref, wd_ref, top)
    half = near_ref.shape[0]
    near_ref[...] = total[:half]
    far_ref[...] = total[half:].astype(far_ref.dtype)


def first_ffn_kernel(mine_ref, *refs, blocks, top):
    ins, (wg_in, wu_in, wd_in, near_ref, far_ref, wg_ref, wu_ref, wd_ref, rows, sems) = refs[:blocks], refs[blocks:]
    pairs = ((wg_in, wg_ref), (wu_in, wu_ref), (wd_in, wd_ref))
    copies = [[pltpu.make_async_copy(a.at[e], b.at[e], sems.at[e, i]) for i, (a, b) in enumerate(pairs)] for e in range(wg_in.shape[0])]
    for row in copies:
        for copy in row:
            copy.start()
    x, meta = gather_rows(ins, rows, near_ref.shape[1])
    total = experts(x, meta, mine_ref, wg_ref, wu_ref, wd_ref, top, lambda e, i: copies[e][i].wait())
    half = near_ref.shape[0]
    near_ref[...] = total[:half]
    far_ref[...] = total[half:].astype(far_ref.dtype)


def ffn(mine, blocks, weights, top, first):
    w_gate, w_up, w_down = weights
    exp_dev, width, hidden = w_gate.shape
    rows = sum(b.shape[0] for b in blocks)
    sums = (
        jax.ShapeDtypeStruct((rows // 2, width), jnp.float32),
        jax.ShapeDtypeStruct((rows // 2, width), jnp.bfloat16),
    )
    scratch = [pltpu.VMEM((rows, blocks[0].shape[1]), jnp.bfloat16)]
    return pl.pallas_call(
        functools.partial(first_ffn_kernel if first else ffn_kernel, blocks=len(blocks), top=top),
        out_shape=sums + (tuple(jax.ShapeDtypeStruct(w.shape, w.dtype) for w in weights) if first else ()),
        in_specs=[VMEM] * (1 + len(blocks)) + [IN_HBM if first else VMEM] * 3,
        out_specs=(VMEM, VMEM) + ((VMEM,) * 3 if first else ()),
        scratch_shapes=scratch + ([pltpu.SemaphoreType.DMA((exp_dev, 3))] if first else []),
        compiler_params=pltpu.CompilerParams(vmem_limit_bytes=(24 if first else 12) << 20),
        cost_estimate=pl.CostEstimate(flops=6 * rows * exp_dev * width * hidden, bytes_accessed=6 * exp_dev * width * hidden, transcendentals=rows * exp_dev * hidden),
        name=f"ffn_first_{rows}" if first else f"ffn_{rows}",
    )(mine, *blocks, *([keep_in_hbm(w) for w in weights] if first else weights))


def join_kernel(near_ref, other_ref, *out_refs):
    step = out_refs[0].shape[0]
    for i, ref in enumerate(out_refs):
        part = near_ref[pl.ds(i * step, step), :] + other_ref[pl.ds(i * step, step), :].astype(jnp.float32)
        ref[...] = part.astype(ref.dtype)


def join(near, other, types):
    step = near.shape[0] // len(types)
    return pl.pallas_call(
        join_kernel,
        out_shape=tuple(jax.ShapeDtypeStruct((step, near.shape[1]), t) for t in types),
        in_specs=[VMEM, VMEM],
        out_specs=(VMEM,) * len(types),
        compiler_params=pltpu.CompilerParams(vmem_limit_bytes=16 << 20),
        name="join",
    )(near, other)


def total_kernel(*refs):
    total = refs[0][...].astype(jnp.float32)
    for ref in refs[1:-1]:
        total += ref[...].astype(jnp.float32)
    refs[-1][...] = total.astype(refs[-1].dtype)


def add_up(parts, dtype):
    return pl.pallas_call(
        total_kernel,
        out_shape=jax.ShapeDtypeStruct(parts[0].shape, dtype),
        in_specs=[VMEM] * len(parts),
        out_specs=VMEM,
        compiler_params=pltpu.CompilerParams(vmem_limit_bytes=16 << 20),
        name="total",
    )(*parts)


def dense(tokens, expert_ids, combine_weights, slot_plan, w_gate, w_up, w_down, cores):
    n_node, n_rank = lax.axis_size("node"), lax.axis_size("rank")
    n_x = n_rank // cores
    exp_dev, width = w_gate.shape[:2]
    top = expert_ids.shape[1]

    def along_z(t, dz):
        return lax.ppermute(t, "node", [(i, i ^ dz) for i in range(n_node)])

    def along_x(t, dx):
        return lax.ppermute(t, "rank", [(i, i ^ (dx * cores)) for i in range(n_rank)])

    def to_chip(t, dz, dx):
        step = dz * n_rank + dx * cores
        return lax.ppermute(t, ("node", "rank"), [(i, i ^ step) for i in range(n_node * n_rank)])

    def swap(t):
        return lax.ppermute(t, "rank", [(i, i ^ 1) for i in range(n_rank)])

    def after(t, *deps):
        return lax.optimization_barrier((t, *deps))[0]

    zs, xs = range(n_node), range(n_x)
    own, mine = prepare(tokens, expert_ids, combine_weights, slot_plan, exp_dev, n_rank)
    near, far, sums, weights = {}, {}, {}, (w_gate, w_up, w_down)

    def run(group, first, *deps):
        blocks = [near[c] for c in group] + [far[c] for c in group]
        return ffn(after(mine, *deps), blocks, weights, top, first)

    def settle(group, keep, give):
        types = [jnp.float32 if dx == 0 and dz != 2 else jnp.bfloat16 for dz, dx in group]
        for c, part in zip(group, join(keep, swap(give), types), strict=True):
            sums[c] = part

    def hop(t, dz):
        for dx in xs[1:]:
            near[dz, dx] = along_x(t, dx)

    near[0, 0] = own
    if n_node > 3:
        near[3, 0] = along_z(own, 3)
    if n_node > 1:
        near[1, 0] = along_z(own, 1)
    hop(own, 0)
    early = [(0, dx) for dx in xs[1:]]
    for dz in zs[2:]:
        if dz != 3:
            near[dz, 0] = along_z(after(own, *[near[c] for c in early]), dz)
    far[0, 0] = swap(own)
    if n_node > 1:
        hop(near[1, 0], 1)
        early += [(1, dx) for dx in xs]
    for c in early:
        far[c] = swap(near[c])
    keep0, give0, *weights = run([(0, 0)], True)
    settle([(0, 0)], keep0, give0)

    column, corner = [(dz, 0) for dz in zs[2:]], [(dz, dx) for dz in zs[2:] for dx in xs[1:]]
    for dz in zs[2:]:
        near[dz, 0] = after(near[dz, 0], give0)
        hop(near[dz, 0], dz)
        far[dz, 0] = swap(near[dz, 0])
    last = give0
    if early:
        keep1, give1 = run(early, False, give0)
        last = give1
    if column:
        keep2, give2 = run(column, False, last)
        last = give2
        for c in corner:
            near[c] = after(near[c], give2)
            far[c] = swap(near[c])
        settle(column, keep2, give2)
    if early:
        settle(early, after(keep1, last), give1)
    if corner:
        keep3, give3 = run(corner, False, *[sums[c] for c in column])
        settle(corner, keep3, give3)

    parts = [sums[0, 0]] + [along_x(sums[0, dx], dx) for dx in xs[1:]]
    for dz in zs[1:]:
        if dz == 2:
            parts += [along_z(sums[dz, 0], dz)] + [to_chip(sums[dz, dx], dz, dx) for dx in xs[1:]]
        else:
            merged = add_up([sums[dz, 0]] + [along_x(sums[dz, dx], dx) for dx in xs[1:]], jnp.bfloat16)
            parts.append(along_z(merged, dz))
    return add_up(parts, tokens.dtype)


def power_of_two(n):
    return n & (n - 1) == 0


def local(tokens, expert_ids, combine_weights, slot_plan, w_gate, w_up, w_down):
    n_node, n_rank = lax.axis_size("node"), lax.axis_size("rank")
    tok_rows, top = expert_ids.shape
    exp_dev = w_gate.shape[0]
    slots = n_node * n_rank * exp_dev
    args = (tokens, expert_ids, combine_weights, slot_plan, w_gate, w_up, w_down)
    sent = exp_dev * capacity_of(tok_rows, top, slots)
    fits = 3 * rounded(top) <= LANES and slots <= 256 and power_of_two(n_node) and power_of_two(n_rank) and n_rank > 1
    if fits and 2 * sent > tok_rows:
        return dense(*args, cores=2)
    return routed(*args)


def solution(mesh):
    in_specs = (
        P(("grp", "node", "rank"), None),
        P(("grp", "node", "rank"), None),
        P(("grp", "node", "rank"), None),
        P(),
        P(("node", "rank"), None, None),
        P(("node", "rank"), None, None),
        P(("node", "rank"), None, None),
    )
    out_specs = P(("grp", "node", "rank"), None)
    return jax.shard_map(local, mesh=mesh, in_specs=in_specs, out_specs=out_specs, check_vma=False)
```

```python
import functools

import jax
import jax.numpy as jnp
from jax import lax
from jax.experimental import pallas as pl
from jax.experimental.pallas import tpu as pltpu
from jax.sharding import PartitionSpec as P

LANES = 128
PIECES = 1
VMEM = pl.BlockSpec(memory_space=pltpu.VMEM)
IN_HBM = pl.BlockSpec(memory_space=pltpu.HBM)


def keep_in_hbm(x):
    return pltpu.with_memory_space_constraint(x, pltpu.HBM)


def capacity_of(tok_rows, top, slots):
    return max(2, (3 * tok_rows * top + 2 * slots - 1) // (2 * slots))


def routed(tokens, expert_ids, combine_weights, slot_plan, w_gate, w_up, w_down):
    n_dev = lax.axis_size("node") * lax.axis_size("rank")
    exp_dev = w_gate.shape[0]
    slots = n_dev * exp_dev
    tok_rows, top = expert_ids.shape
    width = tokens.shape[1]
    capacity = capacity_of(tok_rows, top, slots)
    flat_ids = expert_ids.reshape(-1)
    onehot = (flat_ids[:, None] == jnp.arange(slots, dtype=jnp.int32)[None, :]).astype(jnp.int32)
    slot_of = jnp.sum(onehot * slot_plan[None, :], axis=1)
    earlier = jnp.cumsum(onehot, axis=0) - onehot
    position = jnp.sum(earlier * onehot, axis=1)
    target = slot_of * capacity + position
    repeated = jnp.repeat(tokens, top, axis=0)
    outgoing = jnp.zeros((slots * capacity, width), jnp.bfloat16).at[target].set(repeated)
    flat_out = outgoing.reshape(n_dev, exp_dev * capacity, width)
    arrived = lax.all_to_all(flat_out, ("node", "rank"), split_axis=0, concat_axis=0, tiled=True)
    arrived = arrived.reshape(n_dev, exp_dev, capacity, width)
    gate = jnp.einsum("secd,edf->secf", arrived, w_gate, preferred_element_type=jnp.float32)
    up = jnp.einsum("secd,edf->secf", arrived, w_up, preferred_element_type=jnp.float32)
    hidden = (jax.nn.silu(gate) * up).astype(jnp.bfloat16)
    result = jnp.einsum("secf,efd->secd", hidden, w_down, preferred_element_type=jnp.float32).astype(jnp.bfloat16)
    flat_back = result.reshape(n_dev, exp_dev * capacity, width)
    returned = lax.all_to_all(flat_back, ("node", "rank"), split_axis=0, concat_axis=0, tiled=True)
    returned = returned.reshape(slots * capacity, width)
    picked = returned[target].reshape(tok_rows, top, width)
    scales = combine_weights.astype(jnp.float32) / 65536.0
    mixed = jnp.sum(picked.astype(jnp.float32) * scales[:, :, None], axis=1)
    return mixed.astype(jnp.bfloat16)


def rounded(n):
    return -(-n // 8) * 8


def prepare_kernel(tokens_in, ids_in, weights_in, plan_in, rows_ref, *refs, exp_dev, n_rank):
    mine_ref, ids, weights, meta, plan, sems = refs
    width, top = tokens_in.shape[1], ids.shape[0]
    moves = ((tokens_in, rows_ref.at[:, :width]), (ids_in, ids), (weights_in, weights), (plan_in, plan))
    copies = [pltpu.make_async_copy(a, b, sems.at[i]) for i, (a, b) in enumerate(moves)]
    for copy in copies:
        copy.start()
    device = lax.axis_index("node") * n_rank + lax.axis_index("rank")
    copies[3].wait()
    found = [jnp.int32(0)] * exp_dev
    for expert in range(plan.shape[0]):
        slot = plan[expert]
        found = [jnp.where(slot == device * exp_dev + j, expert, f) for j, f in enumerate(found)]
    lane = lax.broadcasted_iota(jnp.int32, mine_ref.shape, 1)
    mine = jnp.zeros(mine_ref.shape, jnp.int32)
    for j, f in enumerate(found):
        mine = jnp.where(lane == j, f, mine)
    mine_ref[...] = mine.astype(jnp.float32)
    copies[1].wait()
    copies[2].wait()
    w = weights[...]
    meta[...] = jnp.zeros(meta.shape, jnp.float32)
    for i, part in enumerate((ids[...], w // 256, w % 256)):
        meta[pl.ds(i * rounded(top), top), :] = part.astype(jnp.float32)
    rows_ref[:, width:] = meta[...].T.astype(rows_ref.dtype)
    copies[0].wait()


def prepare(tokens, expert_ids, combine_weights, slot_plan, exp_dev, n_rank):
    tok_rows, width = tokens.shape
    args = (tokens, expert_ids.T, combine_weights.T, slot_plan)
    return pl.pallas_call(
        functools.partial(prepare_kernel, exp_dev=exp_dev, n_rank=n_rank),
        out_shape=(
            jax.ShapeDtypeStruct((tok_rows, width + LANES), jnp.bfloat16),
            jax.ShapeDtypeStruct((8, LANES), jnp.float32),
        ),
        in_specs=[IN_HBM] * 4,
        out_specs=(VMEM, VMEM),
        scratch_shapes=[
            pltpu.VMEM(args[1].shape, jnp.int32),
            pltpu.VMEM(args[2].shape, jnp.int32),
            pltpu.VMEM((LANES, tok_rows), jnp.float32),
            pltpu.SMEM(slot_plan.shape, jnp.int32),
            pltpu.SemaphoreType.DMA((4,)),
        ],
        compiler_params=pltpu.CompilerParams(vmem_limit_bytes=8 << 20),
        name="prepare",
    )(*map(keep_in_hbm, args))


def experts(x, meta, mine_ref, wg_ref, wu_ref, wd_ref, top, ready=lambda e, i: None):
    gap = rounded(top)
    ids, high, low = (meta[:, i * gap : i * gap + top] for i in range(3))
    weight = (high * 256.0 + low) * (1.0 / 65536.0)
    total = None
    for e in range(wg_ref.shape[0]):
        scale = jnp.sum(jnp.where(ids == mine_ref[0:1, e : e + 1], weight, 0.0), axis=1, keepdims=True)
        ready(e, 0)
        gate = jnp.dot(x, wg_ref[e], preferred_element_type=jnp.float32)
        ready(e, 1)
        up = jnp.dot(x, wu_ref[e], preferred_element_type=jnp.float32)
        hidden = (gate / (1.0 + jnp.exp(-gate)) * up).astype(jnp.bfloat16)
        ready(e, 2)
        part = jnp.dot(hidden, wd_ref[e], preferred_element_type=jnp.float32) * scale
        total = part if total is None else total + part
    return total


def gather_rows(ins, rows, width):
    start = 0
    for ref in ins:
        rows[pl.ds(start, ref.shape[0]), :] = ref[...]
        start += ref.shape[0]
    return rows[:, :width], rows[:, width:].astype(jnp.float32)


def hand_out(total, near_ref, far_refs):
    half, step = near_ref.shape[0], far_refs[0].shape[0]
    near_ref[...] = total[:half]
    for i, ref in enumerate(far_refs):
        ref[...] = total[half + i * step : half + (i + 1) * step].astype(ref.dtype)


def ffn_kernel(mine_ref, *refs, blocks, top):
    ins, (wg_ref, wu_ref, wd_ref, near_ref, *far_refs, rows) = refs[:blocks], refs[blocks:]
    x, meta = gather_rows(ins, rows, near_ref.shape[1])
    total = experts(x, meta, mine_ref, wg_ref, wu_ref, wd_ref, top)
    hand_out(total, near_ref, far_refs)


def first_ffn_kernel(mine_ref, *refs, blocks, top):
    ins, (wg_in, wu_in, wd_in, near_ref, *far_refs, wg_ref, wu_ref, wd_ref, rows, sems) = refs[:blocks], refs[blocks:]
    pairs = ((wg_in, wg_ref), (wu_in, wu_ref), (wd_in, wd_ref))
    copies = [[pltpu.make_async_copy(a.at[e], b.at[e], sems.at[e, i]) for i, (a, b) in enumerate(pairs)] for e in range(wg_in.shape[0])]
    for row in copies:
        for copy in row:
            copy.start()
    x, meta = gather_rows(ins, rows, near_ref.shape[1])
    total = experts(x, meta, mine_ref, wg_ref, wu_ref, wd_ref, top, lambda e, i: copies[e][i].wait())
    hand_out(total, near_ref, far_refs)


def ffn(mine, blocks, weights, top, first, pieces):
    w_gate, w_up, w_down = weights
    exp_dev, width, hidden = w_gate.shape
    rows = sum(b.shape[0] for b in blocks)
    sums = (jax.ShapeDtypeStruct((rows // 2, width), jnp.float32),)
    sums += (jax.ShapeDtypeStruct((rows // 2 // pieces, width), jnp.bfloat16),) * pieces
    scratch = [pltpu.VMEM((rows, blocks[0].shape[1]), jnp.bfloat16)]
    return pl.pallas_call(
        functools.partial(first_ffn_kernel if first else ffn_kernel, blocks=len(blocks), top=top),
        out_shape=sums + (tuple(jax.ShapeDtypeStruct(w.shape, w.dtype) for w in weights) if first else ()),
        in_specs=[VMEM] * (1 + len(blocks)) + [IN_HBM if first else VMEM] * 3,
        out_specs=(VMEM,) * (1 + pieces + (3 if first else 0)),
        scratch_shapes=scratch + ([pltpu.SemaphoreType.DMA((exp_dev, 3))] if first else []),
        compiler_params=pltpu.CompilerParams(vmem_limit_bytes=(24 if first else 12) << 20),
        cost_estimate=pl.CostEstimate(flops=6 * rows * exp_dev * width * hidden, bytes_accessed=6 * exp_dev * width * hidden, transcendentals=rows * exp_dev * hidden),
        name=f"ffn_first_{rows}" if first else f"ffn_{rows}",
    )(mine, *blocks, *([keep_in_hbm(w) for w in weights] if first else weights))


def join_kernel(near_ref, *refs, pieces):
    others, out_refs = refs[:pieces], refs[pieces:]
    step = out_refs[0].shape[0]
    other = jnp.concatenate([ref[...] for ref in others], axis=0) if pieces > 1 else others[0][...]
    for i, ref in enumerate(out_refs):
        part = near_ref[pl.ds(i * step, step), :] + other[i * step : (i + 1) * step, :].astype(jnp.float32)
        ref[...] = part.astype(ref.dtype)


def join(near, others, types):
    step = near.shape[0] // len(types)
    return pl.pallas_call(
        functools.partial(join_kernel, pieces=len(others)),
        out_shape=tuple(jax.ShapeDtypeStruct((step, near.shape[1]), t) for t in types),
        in_specs=[VMEM] * (1 + len(others)),
        out_specs=(VMEM,) * len(types),
        compiler_params=pltpu.CompilerParams(vmem_limit_bytes=16 << 20),
        name=f"join_{near.shape[0]}",
    )(near, *others)


def total_kernel(*refs):
    total = refs[0][...].astype(jnp.float32)
    for ref in refs[1:-1]:
        total += ref[...].astype(jnp.float32)
    refs[-1][...] = total.astype(refs[-1].dtype)


def add_up(parts, dtype, flops=None):
    return pl.pallas_call(
        total_kernel,
        out_shape=jax.ShapeDtypeStruct(parts[0].shape, dtype),
        in_specs=[VMEM] * len(parts),
        out_specs=VMEM,
        compiler_params=pltpu.CompilerParams(vmem_limit_bytes=16 << 20),
        cost_estimate=flops and pl.CostEstimate(flops=flops, bytes_accessed=flops // 100, transcendentals=0),
        name="total",
    )(*parts)


def dense(tokens, expert_ids, combine_weights, slot_plan, w_gate, w_up, w_down, cores):
    n_node, n_rank = lax.axis_size("node"), lax.axis_size("rank")
    n_x = n_rank // cores
    exp_dev, width = w_gate.shape[:2]
    top = expert_ids.shape[1]

    def along_x(t, dx):
        return lax.ppermute(t, "rank", [(i, i ^ (dx * cores)) for i in range(n_rank)])

    def to_chip(t, dz, dx):
        if dz == 0:
            return along_x(t, dx)
        if dx == 0:
            return lax.ppermute(t, "node", [(i, i ^ dz) for i in range(n_node)])
        step = dz * n_rank + dx * cores
        return lax.ppermute(t, ("node", "rank"), [(i, i ^ step) for i in range(n_node * n_rank)])

    def swap(t):
        return lax.ppermute(t, "rank", [(i, i ^ 1) for i in range(n_rank)])

    def after(t, *deps):
        return lax.optimization_barrier((t, *deps))[0]

    zs, xs = range(n_node), range(n_x)
    own, mine = prepare(tokens, expert_ids, combine_weights, slot_plan, exp_dev, n_rank)
    near, far, sums, weights = {}, {}, {}, (w_gate, w_up, w_down)

    def run(group, last, pieces=1):
        blocks = sum([near[c] for c in group] + [far[c] for c in group], [])
        keep, *give = ffn(after(mine, *last), blocks, weights, top, weights[0] is w_gate, pieces)
        return keep, give[:pieces], give[pieces:] or weights

    def settle(group, keep, others, wide):
        types = [jnp.float32 if c in wide else jnp.bfloat16 for c in group]
        for c, part in zip(group, join(keep, others, types), strict=True):
            sums[c] = part

    home, across = [(0, 0)], [(0, dx) for dx in xs[1:]]
    column, corner = [(dz, 0) for dz in zs[2:]], [(dz, dx) for dz in zs[2:] for dx in xs[1:]]
    close = [(dz, dx) for dz in zs[1:2] for dx in xs]
    wide = home + [(dz, 0) for dz in zs[1:] if dz != 2]

    near[0, 0] = [own]
    for c in across + close + column:
        near[c] = [to_chip(own, *c)]
    far[0, 0] = [swap(own)]
    keep, give, weights = run(home, [])
    settle(home, keep, [swap(t) for t in give], wide)
    names = across + close + column
    near |= dict(zip(names, after([near[c] for c in names], give), strict=True))

    for dz, _ in reversed(column):
        for dx in xs[1:]:
            near[dz, dx] = [along_x(t, dx) for t in near[dz, 0]]
    for c in names:
        far[c] = [swap(t) for t in near[c]]
    last, waits = give, []
    for group in (column, across + close, corner):
        if not group:
            continue
        if group is corner:
            for c in group:
                near[c] = after(near[c], last)
                far[c] = [swap(t) for t in near[c]]
        keep, last, _ = run(group, last + (waits if group is corner else []))
        settle(group, keep, [swap(t) for t in last], wide)
        if group is column:
            waits = [sums[c] for c in group]

    def send(c):
        more = [along_x(sums[c[0], dx], dx) for dx in xs[1:]] if c[0] not in (0, 2) else []
        return to_chip(add_up([sums[c]] + more, jnp.bfloat16) if more else sums[c], *c)

    early = [(dz, dx) for dz in zs[2:3] for dx in xs] + across
    late = [c for c in across + [(dz, 0) for dz in zs[1:]] if c not in early]
    part = add_up([sums[0, 0]] + [send(c) for c in early], jnp.float32, 10**10) if early else sums[0, 0]
    return add_up([part] + [send(c) for c in late], tokens.dtype)


def power_of_two(n):
    return n & (n - 1) == 0


def local(tokens, expert_ids, combine_weights, slot_plan, w_gate, w_up, w_down):
    n_node, n_rank = lax.axis_size("node"), lax.axis_size("rank")
    tok_rows, top = expert_ids.shape
    exp_dev = w_gate.shape[0]
    slots = n_node * n_rank * exp_dev
    args = (tokens, expert_ids, combine_weights, slot_plan, w_gate, w_up, w_down)
    sent = exp_dev * capacity_of(tok_rows, top, slots)
    fits = 3 * rounded(top) <= LANES and slots <= 256 and power_of_two(n_node) and power_of_two(n_rank) and n_rank > 1
    if fits and 2 * sent > tok_rows:
        return dense(*args, cores=2)
    return routed(*args)


def solution(mesh):
    in_specs = (
        P(("grp", "node", "rank"), None),
        P(("grp", "node", "rank"), None),
        P(("grp", "node", "rank"), None),
        P(),
        P(("node", "rank"), None, None),
        P(("node", "rank"), None, None),
        P(("node", "rank"), None, None),
    )
    out_specs = P(("grp", "node", "rank"), None)
    return jax.shard_map(local, mesh=mesh, in_specs=in_specs, out_specs=out_specs, check_vma=False)
```

```python
import functools

import jax
import jax.numpy as jnp
from jax import lax
from jax.experimental import pallas as pl
from jax.experimental.pallas import tpu as pltpu
from jax.sharding import PartitionSpec as P

LANES = 128
PIECES = 1
VMEM = pl.BlockSpec(memory_space=pltpu.VMEM)
IN_HBM = pl.BlockSpec(memory_space=pltpu.HBM)


def keep_in_hbm(x):
    return pltpu.with_memory_space_constraint(x, pltpu.HBM)


def capacity_of(tok_rows, top, slots):
    return max(2, (3 * tok_rows * top + 2 * slots - 1) // (2 * slots))


def routed(tokens, expert_ids, combine_weights, slot_plan, w_gate, w_up, w_down):
    n_dev = lax.axis_size("node") * lax.axis_size("rank")
    exp_dev = w_gate.shape[0]
    slots = n_dev * exp_dev
    tok_rows, top = expert_ids.shape
    width = tokens.shape[1]
    capacity = capacity_of(tok_rows, top, slots)
    flat_ids = expert_ids.reshape(-1)
    onehot = (flat_ids[:, None] == jnp.arange(slots, dtype=jnp.int32)[None, :]).astype(jnp.int32)
    slot_of = jnp.sum(onehot * slot_plan[None, :], axis=1)
    earlier = jnp.cumsum(onehot, axis=0) - onehot
    position = jnp.sum(earlier * onehot, axis=1)
    target = slot_of * capacity + position
    repeated = jnp.repeat(tokens, top, axis=0)
    outgoing = jnp.zeros((slots * capacity, width), jnp.bfloat16).at[target].set(repeated)
    flat_out = outgoing.reshape(n_dev, exp_dev * capacity, width)
    arrived = lax.all_to_all(flat_out, ("node", "rank"), split_axis=0, concat_axis=0, tiled=True)
    arrived = arrived.reshape(n_dev, exp_dev, capacity, width)
    gate = jnp.einsum("secd,edf->secf", arrived, w_gate, preferred_element_type=jnp.float32)
    up = jnp.einsum("secd,edf->secf", arrived, w_up, preferred_element_type=jnp.float32)
    hidden = (jax.nn.silu(gate) * up).astype(jnp.bfloat16)
    result = jnp.einsum("secf,efd->secd", hidden, w_down, preferred_element_type=jnp.float32).astype(jnp.bfloat16)
    flat_back = result.reshape(n_dev, exp_dev * capacity, width)
    returned = lax.all_to_all(flat_back, ("node", "rank"), split_axis=0, concat_axis=0, tiled=True)
    returned = returned.reshape(slots * capacity, width)
    picked = returned[target].reshape(tok_rows, top, width)
    scales = combine_weights.astype(jnp.float32) / 65536.0
    mixed = jnp.sum(picked.astype(jnp.float32) * scales[:, :, None], axis=1)
    return mixed.astype(jnp.bfloat16)


def rounded(n):
    return -(-n // 8) * 8


def prepare_kernel(tokens_in, ids_in, weights_in, plan_in, rows_ref, *refs, exp_dev, n_rank):
    mine_ref, ids, weights, meta, plan, sems = refs
    width, top = tokens_in.shape[1], ids.shape[0]
    moves = ((tokens_in, rows_ref.at[:, :width]), (ids_in, ids), (weights_in, weights), (plan_in, plan))
    copies = [pltpu.make_async_copy(a, b, sems.at[i]) for i, (a, b) in enumerate(moves)]
    for copy in copies:
        copy.start()
    device = lax.axis_index("node") * n_rank + lax.axis_index("rank")
    copies[3].wait()
    found = [jnp.int32(0)] * exp_dev
    for expert in range(plan.shape[0]):
        slot = plan[expert]
        found = [jnp.where(slot == device * exp_dev + j, expert, f) for j, f in enumerate(found)]
    lane = lax.broadcasted_iota(jnp.int32, mine_ref.shape, 1)
    mine = jnp.zeros(mine_ref.shape, jnp.int32)
    for j, f in enumerate(found):
        mine = jnp.where(lane == j, f, mine)
    mine_ref[...] = mine.astype(jnp.float32)
    copies[1].wait()
    copies[2].wait()
    w = weights[...]
    meta[...] = jnp.zeros(meta.shape, jnp.float32)
    for i, part in enumerate((ids[...], w // 256, w % 256)):
        meta[pl.ds(i * rounded(top), top), :] = part.astype(jnp.float32)
    rows_ref[:, width:] = meta[...].T.astype(rows_ref.dtype)
    copies[0].wait()


def prepare(tokens, expert_ids, combine_weights, slot_plan, exp_dev, n_rank):
    tok_rows, width = tokens.shape
    args = (tokens, expert_ids.T, combine_weights.T, slot_plan)
    return pl.pallas_call(
        functools.partial(prepare_kernel, exp_dev=exp_dev, n_rank=n_rank),
        out_shape=(
            jax.ShapeDtypeStruct((tok_rows, width + LANES), jnp.bfloat16),
            jax.ShapeDtypeStruct((8, LANES), jnp.float32),
        ),
        in_specs=[IN_HBM] * 4,
        out_specs=(VMEM, VMEM),
        scratch_shapes=[
            pltpu.VMEM(args[1].shape, jnp.int32),
            pltpu.VMEM(args[2].shape, jnp.int32),
            pltpu.VMEM((LANES, tok_rows), jnp.float32),
            pltpu.SMEM(slot_plan.shape, jnp.int32),
            pltpu.SemaphoreType.DMA((4,)),
        ],
        compiler_params=pltpu.CompilerParams(vmem_limit_bytes=8 << 20),
        name="prepare",
    )(*map(keep_in_hbm, args))


def experts(x, meta, mine_ref, wg_ref, wu_ref, wd_ref, top, ready=lambda e, i: None):
    gap = rounded(top)
    ids, high, low = (meta[:, i * gap : i * gap + top] for i in range(3))
    weight = (high * 256.0 + low) * (1.0 / 65536.0)
    total = None
    for e in range(wg_ref.shape[0]):
        scale = jnp.sum(jnp.where(ids == mine_ref[0:1, e : e + 1], weight, 0.0), axis=1, keepdims=True)
        ready(e, 0)
        gate = jnp.dot(x, wg_ref[e], preferred_element_type=jnp.float32)
        ready(e, 1)
        up = jnp.dot(x, wu_ref[e], preferred_element_type=jnp.float32)
        hidden = (gate / (1.0 + jnp.exp(-gate)) * up).astype(jnp.bfloat16)
        ready(e, 2)
        part = jnp.dot(hidden, wd_ref[e], preferred_element_type=jnp.float32) * scale
        total = part if total is None else total + part
    return total


def gather_rows(ins, rows, width):
    start = 0
    for ref in ins:
        rows[pl.ds(start, ref.shape[0]), :] = ref[...]
        start += ref.shape[0]
    return rows[:, :width], rows[:, width:].astype(jnp.float32)


def hand_out(total, near_ref, far_refs):
    half, step = near_ref.shape[0], far_refs[0].shape[0]
    near_ref[...] = total[:half]
    for i, ref in enumerate(far_refs):
        ref[...] = total[half + i * step : half + (i + 1) * step].astype(ref.dtype)


def ffn_kernel(mine_ref, *refs, blocks, top):
    ins, (wg_ref, wu_ref, wd_ref, near_ref, *far_refs, rows) = refs[:blocks], refs[blocks:]
    x, meta = gather_rows(ins, rows, near_ref.shape[1])
    total = experts(x, meta, mine_ref, wg_ref, wu_ref, wd_ref, top)
    hand_out(total, near_ref, far_refs)


def first_ffn_kernel(mine_ref, *refs, blocks, top):
    ins, (wg_in, wu_in, wd_in, near_ref, *far_refs, wg_ref, wu_ref, wd_ref, rows, sems) = refs[:blocks], refs[blocks:]
    pairs = ((wg_in, wg_ref), (wu_in, wu_ref), (wd_in, wd_ref))
    copies = [[pltpu.make_async_copy(a.at[e], b.at[e], sems.at[e, i]) for i, (a, b) in enumerate(pairs)] for e in range(wg_in.shape[0])]
    for row in copies:
        for copy in row:
            copy.start()
    x, meta = gather_rows(ins, rows, near_ref.shape[1])
    total = experts(x, meta, mine_ref, wg_ref, wu_ref, wd_ref, top, lambda e, i: copies[e][i].wait())
    hand_out(total, near_ref, far_refs)


def ffn(mine, blocks, weights, top, first, pieces):
    w_gate, w_up, w_down = weights
    exp_dev, width, hidden = w_gate.shape
    rows = sum(b.shape[0] for b in blocks)
    sums = (jax.ShapeDtypeStruct((rows // 2, width), jnp.float32),)
    sums += (jax.ShapeDtypeStruct((rows // 2 // pieces, width), jnp.bfloat16),) * pieces
    scratch = [pltpu.VMEM((rows, blocks[0].shape[1]), jnp.bfloat16)]
    return pl.pallas_call(
        functools.partial(first_ffn_kernel if first else ffn_kernel, blocks=len(blocks), top=top),
        out_shape=sums + (tuple(jax.ShapeDtypeStruct(w.shape, w.dtype) for w in weights) if first else ()),
        in_specs=[VMEM] * (1 + len(blocks)) + [IN_HBM if first else VMEM] * 3,
        out_specs=(VMEM,) * (1 + pieces + (3 if first else 0)),
        scratch_shapes=scratch + ([pltpu.SemaphoreType.DMA((exp_dev, 3))] if first else []),
        compiler_params=pltpu.CompilerParams(vmem_limit_bytes=(24 if first else 12) << 20),
        cost_estimate=pl.CostEstimate(flops=6 * rows * exp_dev * width * hidden, bytes_accessed=6 * exp_dev * width * hidden, transcendentals=rows * exp_dev * hidden),
        name=f"ffn_first_{rows}" if first else f"ffn_{rows}",
    )(mine, *blocks, *([keep_in_hbm(w) for w in weights] if first else weights))


def join_kernel(near_ref, *refs, pieces):
    others, out_refs = refs[:pieces], refs[pieces:]
    step = out_refs[0].shape[0]
    other = jnp.concatenate([ref[...] for ref in others], axis=0) if pieces > 1 else others[0][...]
    for i, ref in enumerate(out_refs):
        part = near_ref[pl.ds(i * step, step), :] + other[i * step : (i + 1) * step, :].astype(jnp.float32)
        ref[...] = part.astype(ref.dtype)


def join(near, others, types):
    step = near.shape[0] // len(types)
    return pl.pallas_call(
        functools.partial(join_kernel, pieces=len(others)),
        out_shape=tuple(jax.ShapeDtypeStruct((step, near.shape[1]), t) for t in types),
        in_specs=[VMEM] * (1 + len(others)),
        out_specs=(VMEM,) * len(types),
        compiler_params=pltpu.CompilerParams(vmem_limit_bytes=16 << 20),
        name=f"join_{near.shape[0]}",
    )(near, *others)


def total_kernel(*refs):
    total = refs[0][...].astype(jnp.float32)
    for ref in refs[1:-1]:
        total += ref[...].astype(jnp.float32)
    refs[-1][...] = total.astype(refs[-1].dtype)


def add_up(parts, dtype, flops=None):
    return pl.pallas_call(
        total_kernel,
        out_shape=jax.ShapeDtypeStruct(parts[0].shape, dtype),
        in_specs=[VMEM] * len(parts),
        out_specs=VMEM,
        compiler_params=pltpu.CompilerParams(vmem_limit_bytes=16 << 20),
        cost_estimate=flops and pl.CostEstimate(flops=flops, bytes_accessed=flops // 100, transcendentals=0),
        name="total",
    )(*parts)


def dense(tokens, expert_ids, combine_weights, slot_plan, w_gate, w_up, w_down, cores):
    n_node, n_rank = lax.axis_size("node"), lax.axis_size("rank")
    n_x = n_rank // cores
    exp_dev, width = w_gate.shape[:2]
    top = expert_ids.shape[1]

    def along_x(t, dx):
        return lax.ppermute(t, "rank", [(i, i ^ (dx * cores)) for i in range(n_rank)])

    def to_chip(t, dz, dx):
        if dz == 0:
            return along_x(t, dx)
        if dx == 0:
            return lax.ppermute(t, "node", [(i, i ^ dz) for i in range(n_node)])
        step = dz * n_rank + dx * cores
        return lax.ppermute(t, ("node", "rank"), [(i, i ^ step) for i in range(n_node * n_rank)])

    def swap(t):
        return lax.ppermute(t, "rank", [(i, i ^ 1) for i in range(n_rank)])

    def after(t, *deps):
        return lax.optimization_barrier((t, *deps))[0]

    zs, xs = range(n_node), range(n_x)
    own, mine = prepare(tokens, expert_ids, combine_weights, slot_plan, exp_dev, n_rank)
    near, far, sums, weights = {}, {}, {}, (w_gate, w_up, w_down)

    def run(group, last, pieces=1):
        blocks = sum([near[c] for c in group] + [far[c] for c in group], [])
        keep, *give = ffn(after(mine, *last), blocks, weights, top, weights[0] is w_gate, pieces)
        return keep, give[:pieces], give[pieces:] or weights

    def settle(group, keep, others, wide):
        types = [jnp.float32 if c in wide else jnp.bfloat16 for c in group]
        for c, part in zip(group, join(keep, others, types), strict=True):
            sums[c] = part

    home, across = [(0, 0)], [(0, dx) for dx in xs[1:]]
    column, corner = [(dz, 0) for dz in zs[2:]], [(dz, dx) for dz in zs[2:] for dx in xs[1:]]
    close = [(dz, dx) for dz in zs[1:2] for dx in xs]
    wide = home + [(dz, 0) for dz in zs[1:] if dz != 2]

    near[0, 0] = [own]
    for c in across + close + column:
        near[c] = [to_chip(own, *c)]
    far[0, 0] = [swap(own)]
    keep, give, weights = run(home, [])
    settle(home, keep, [swap(t) for t in give], wide)
    names = across + close + column
    near |= dict(zip(names, after([near[c] for c in names], give), strict=True))

    for dz, _ in reversed(column):
        for dx in xs[1:]:
            near[dz, dx] = [along_x(t, dx) for t in near[dz, 0]]
    for c in column + across + close:
        far[c] = [swap(t) for t in near[c]]
    last, waits = give, []
    for group in (column, across + close, corner):
        if not group:
            continue
        if group is corner:
            for c in group:
                near[c] = after(near[c], last)
                far[c] = [swap(t) for t in near[c]]
        keep, last, _ = run(group, last + (waits if group is corner else []))
        settle(group, keep, [swap(t) for t in last], wide)
        if group is column:
            waits = [sums[c] for c in group]

    def send(c):
        more = [along_x(sums[c[0], dx], dx) for dx in xs[1:]] if c[0] not in (0, 2) else []
        return to_chip(add_up([sums[c]] + more, jnp.bfloat16, None) if more else sums[c], *c)

    early = [(2, 0)] + [(2, dx) for dx in xs[1:]] + across
    late = [c for c in across + [(dz, 0) for dz in zs[1:]] if c not in early]
    part = add_up([sums[0, 0]] + [send(c) for c in early], jnp.float32, 10000000000) if early else sums[0, 0]
    late = late[::-1]
    return add_up([part] + [send(c) for c in late], tokens.dtype)


def power_of_two(n):
    return n & (n - 1) == 0


def local(tokens, expert_ids, combine_weights, slot_plan, w_gate, w_up, w_down):
    n_node, n_rank = lax.axis_size("node"), lax.axis_size("rank")
    tok_rows, top = expert_ids.shape
    exp_dev = w_gate.shape[0]
    slots = n_node * n_rank * exp_dev
    args = (tokens, expert_ids, combine_weights, slot_plan, w_gate, w_up, w_down)
    sent = exp_dev * capacity_of(tok_rows, top, slots)
    fits = 3 * rounded(top) <= LANES and slots <= 256 and power_of_two(n_node) and power_of_two(n_rank) and n_rank > 1
    if fits and 2 * sent > tok_rows:
        return dense(*args, cores=2)
    return routed(*args)


def solution(mesh):
    in_specs = (
        P(("grp", "node", "rank"), None),
        P(("grp", "node", "rank"), None),
        P(("grp", "node", "rank"), None),
        P(),
        P(("node", "rank"), None, None),
        P(("node", "rank"), None, None),
        P(("node", "rank"), None, None),
    )
    out_specs = P(("grp", "node", "rank"), None)
    return jax.shard_map(local, mesh=mesh, in_specs=in_specs, out_specs=out_specs, check_vma=False)
```

```python
import functools

import jax
import jax.numpy as jnp
from jax import lax
from jax.experimental import pallas as pl
from jax.experimental.pallas import tpu as pltpu
from jax.sharding import PartitionSpec as P

LANES = 128
PIECES = 1
VMEM = pl.BlockSpec(memory_space=pltpu.VMEM)
IN_HBM = pl.BlockSpec(memory_space=pltpu.HBM)


def keep_in_hbm(x):
    return pltpu.with_memory_space_constraint(x, pltpu.HBM)


def capacity_of(tok_rows, top, slots):
    return max(2, (3 * tok_rows * top + 2 * slots - 1) // (2 * slots))


def routed(tokens, expert_ids, combine_weights, slot_plan, w_gate, w_up, w_down):
    n_dev = lax.axis_size("node") * lax.axis_size("rank")
    exp_dev = w_gate.shape[0]
    slots = n_dev * exp_dev
    tok_rows, top = expert_ids.shape
    width = tokens.shape[1]
    capacity = capacity_of(tok_rows, top, slots)
    flat_ids = expert_ids.reshape(-1)
    onehot = (flat_ids[:, None] == jnp.arange(slots, dtype=jnp.int32)[None, :]).astype(jnp.int32)
    slot_of = jnp.sum(onehot * slot_plan[None, :], axis=1)
    earlier = jnp.cumsum(onehot, axis=0) - onehot
    position = jnp.sum(earlier * onehot, axis=1)
    target = slot_of * capacity + position
    repeated = jnp.repeat(tokens, top, axis=0)
    outgoing = jnp.zeros((slots * capacity, width), jnp.bfloat16).at[target].set(repeated)
    flat_out = outgoing.reshape(n_dev, exp_dev * capacity, width)
    arrived = lax.all_to_all(flat_out, ("node", "rank"), split_axis=0, concat_axis=0, tiled=True)
    arrived = arrived.reshape(n_dev, exp_dev, capacity, width)
    gate = jnp.einsum("secd,edf->secf", arrived, w_gate, preferred_element_type=jnp.float32)
    up = jnp.einsum("secd,edf->secf", arrived, w_up, preferred_element_type=jnp.float32)
    hidden = (jax.nn.silu(gate) * up).astype(jnp.bfloat16)
    result = jnp.einsum("secf,efd->secd", hidden, w_down, preferred_element_type=jnp.float32).astype(jnp.bfloat16)
    flat_back = result.reshape(n_dev, exp_dev * capacity, width)
    returned = lax.all_to_all(flat_back, ("node", "rank"), split_axis=0, concat_axis=0, tiled=True)
    returned = returned.reshape(slots * capacity, width)
    picked = returned[target].reshape(tok_rows, top, width)
    scales = combine_weights.astype(jnp.float32) / 65536.0
    mixed = jnp.sum(picked.astype(jnp.float32) * scales[:, :, None], axis=1)
    return mixed.astype(jnp.bfloat16)


def rounded(n):
    return -(-n // 8) * 8


def prepare_kernel(tokens_in, ids_in, weights_in, plan_in, rows_ref, *refs, exp_dev, n_rank):
    mine_ref, ids, weights, meta, plan, sems = refs
    width, top = tokens_in.shape[1], ids.shape[0]
    moves = ((tokens_in, rows_ref.at[:, :width]), (ids_in, ids), (weights_in, weights), (plan_in, plan))
    copies = [pltpu.make_async_copy(a, b, sems.at[i]) for i, (a, b) in enumerate(moves)]
    for copy in copies:
        copy.start()
    device = lax.axis_index("node") * n_rank + lax.axis_index("rank")
    copies[3].wait()
    found = [jnp.int32(0)] * exp_dev
    for expert in range(plan.shape[0]):
        slot = plan[expert]
        found = [jnp.where(slot == device * exp_dev + j, expert, f) for j, f in enumerate(found)]
    lane = lax.broadcasted_iota(jnp.int32, mine_ref.shape, 1)
    mine = jnp.zeros(mine_ref.shape, jnp.int32)
    for j, f in enumerate(found):
        mine = jnp.where(lane == j, f, mine)
    mine_ref[...] = mine.astype(jnp.float32)
    copies[1].wait()
    copies[2].wait()
    w = weights[...]
    meta[...] = jnp.zeros(meta.shape, jnp.float32)
    for i, part in enumerate((ids[...], w // 256, w % 256)):
        meta[pl.ds(i * rounded(top), top), :] = part.astype(jnp.float32)
    rows_ref[:, width:] = meta[...].T.astype(rows_ref.dtype)
    copies[0].wait()


def prepare(tokens, expert_ids, combine_weights, slot_plan, exp_dev, n_rank):
    tok_rows, width = tokens.shape
    args = (tokens, expert_ids.T, combine_weights.T, slot_plan)
    return pl.pallas_call(
        functools.partial(prepare_kernel, exp_dev=exp_dev, n_rank=n_rank),
        out_shape=(
            jax.ShapeDtypeStruct((tok_rows, width + LANES), jnp.bfloat16),
            jax.ShapeDtypeStruct((8, LANES), jnp.float32),
        ),
        in_specs=[IN_HBM] * 4,
        out_specs=(VMEM, VMEM),
        scratch_shapes=[
            pltpu.VMEM(args[1].shape, jnp.int32),
            pltpu.VMEM(args[2].shape, jnp.int32),
            pltpu.VMEM((LANES, tok_rows), jnp.float32),
            pltpu.SMEM(slot_plan.shape, jnp.int32),
            pltpu.SemaphoreType.DMA((4,)),
        ],
        compiler_params=pltpu.CompilerParams(vmem_limit_bytes=8 << 20),
        name="prepare",
    )(*map(keep_in_hbm, args))


def experts(x, meta, mine_ref, wg_ref, wu_ref, wd_ref, top, ready=lambda e, i: None):
    gap = rounded(top)
    ids, high, low = (meta[:, i * gap : i * gap + top] for i in range(3))
    weight = (high * 256.0 + low) * (1.0 / 65536.0)
    hidden = []
    for e in range(wg_ref.shape[0]):
        scale = jnp.sum(jnp.where(ids == mine_ref[0:1, e : e + 1], weight, 0.0), axis=1, keepdims=True)
        ready(e, 0)
        gate = jnp.dot(x, wg_ref[e], preferred_element_type=jnp.float32)
        ready(e, 1)
        up = jnp.dot(x, wu_ref[e], preferred_element_type=jnp.float32)
        hidden.append((gate / (1.0 + jnp.exp(-gate)) * up * scale).astype(jnp.bfloat16))
    for e in range(wd_ref.shape[0]):
        ready(e, 2)
    down = wd_ref[...].reshape(-1, wd_ref.shape[2])
    return jnp.dot(jnp.concatenate(hidden, axis=1), down, preferred_element_type=jnp.float32)


def gather_rows(ins, rows, width):
    start = 0
    for ref in ins:
        rows[pl.ds(start, ref.shape[0]), :] = ref[...]
        start += ref.shape[0]
    return rows[:, :width], rows[:, width:].astype(jnp.float32)


def hand_out(total, near_ref, far_refs):
    half, step = near_ref.shape[0], far_refs[0].shape[0]
    near_ref[...] = total[:half]
    for i, ref in enumerate(far_refs):
        ref[...] = total[half + i * step : half + (i + 1) * step].astype(ref.dtype)


def ffn_kernel(mine_ref, *refs, blocks, top):
    ins, (wg_ref, wu_ref, wd_ref, near_ref, *far_refs, rows) = refs[:blocks], refs[blocks:]
    x, meta = gather_rows(ins, rows, near_ref.shape[1])
    total = experts(x, meta, mine_ref, wg_ref, wu_ref, wd_ref, top)
    hand_out(total, near_ref, far_refs)


def first_ffn_kernel(mine_ref, *refs, blocks, top):
    ins, (wg_in, wu_in, wd_in, near_ref, *far_refs, wg_ref, wu_ref, wd_ref, rows, sems) = refs[:blocks], refs[blocks:]
    pairs = ((wg_in, wg_ref), (wu_in, wu_ref), (wd_in, wd_ref))
    copies = [[pltpu.make_async_copy(a.at[e], b.at[e], sems.at[e, i]) for i, (a, b) in enumerate(pairs)] for e in range(wg_in.shape[0])]
    for row in copies:
        for copy in row:
            copy.start()
    x, meta = gather_rows(ins, rows, near_ref.shape[1])
    total = experts(x, meta, mine_ref, wg_ref, wu_ref, wd_ref, top, lambda e, i: copies[e][i].wait())
    hand_out(total, near_ref, far_refs)


def ffn(mine, blocks, weights, top, first, pieces):
    w_gate, w_up, w_down = weights
    exp_dev, width, hidden = w_gate.shape
    rows = sum(b.shape[0] for b in blocks)
    sums = (jax.ShapeDtypeStruct((rows // 2, width), jnp.float32),)
    sums += (jax.ShapeDtypeStruct((rows // 2 // pieces, width), jnp.bfloat16),) * pieces
    scratch = [pltpu.VMEM((rows, blocks[0].shape[1]), jnp.bfloat16)]
    return pl.pallas_call(
        functools.partial(first_ffn_kernel if first else ffn_kernel, blocks=len(blocks), top=top),
        out_shape=sums + (tuple(jax.ShapeDtypeStruct(w.shape, w.dtype) for w in weights) if first else ()),
        in_specs=[VMEM] * (1 + len(blocks)) + [IN_HBM if first else VMEM] * 3,
        out_specs=(VMEM,) * (1 + pieces + (3 if first else 0)),
        scratch_shapes=scratch + ([pltpu.SemaphoreType.DMA((exp_dev, 3))] if first else []),
        compiler_params=pltpu.CompilerParams(vmem_limit_bytes=(24 if first else 12) << 20),
        cost_estimate=pl.CostEstimate(flops=6 * rows * exp_dev * width * hidden, bytes_accessed=6 * exp_dev * width * hidden, transcendentals=rows * exp_dev * hidden),
        name=f"ffn_first_{rows}" if first else f"ffn_{rows}",
    )(mine, *blocks, *([keep_in_hbm(w) for w in weights] if first else weights))


def join_kernel(near_ref, *refs, pieces):
    others, out_refs = refs[:pieces], refs[pieces:]
    step = out_refs[0].shape[0]
    other = jnp.concatenate([ref[...] for ref in others], axis=0) if pieces > 1 else others[0][...]
    for i, ref in enumerate(out_refs):
        part = near_ref[pl.ds(i * step, step), :] + other[i * step : (i + 1) * step, :].astype(jnp.float32)
        ref[...] = part.astype(ref.dtype)


def join(near, others, types):
    step = near.shape[0] // len(types)
    return pl.pallas_call(
        functools.partial(join_kernel, pieces=len(others)),
        out_shape=tuple(jax.ShapeDtypeStruct((step, near.shape[1]), t) for t in types),
        in_specs=[VMEM] * (1 + len(others)),
        out_specs=(VMEM,) * len(types),
        compiler_params=pltpu.CompilerParams(vmem_limit_bytes=16 << 20),
        name=f"join_{near.shape[0]}",
    )(near, *others)


def total_kernel(*refs):
    total = refs[0][...].astype(jnp.float32)
    for ref in refs[1:-1]:
        total += ref[...].astype(jnp.float32)
    refs[-1][...] = total.astype(refs[-1].dtype)


def add_up(parts, dtype, flops=None):
    return pl.pallas_call(
        total_kernel,
        out_shape=jax.ShapeDtypeStruct(parts[0].shape, dtype),
        in_specs=[VMEM] * len(parts),
        out_specs=VMEM,
        compiler_params=pltpu.CompilerParams(vmem_limit_bytes=16 << 20),
        cost_estimate=flops and pl.CostEstimate(flops=flops, bytes_accessed=flops // 100, transcendentals=0),
        name="total",
    )(*parts)


def dense(tokens, expert_ids, combine_weights, slot_plan, w_gate, w_up, w_down, cores):
    n_node, n_rank = lax.axis_size("node"), lax.axis_size("rank")
    n_x = n_rank // cores
    exp_dev, width = w_gate.shape[:2]
    top = expert_ids.shape[1]

    def along_x(t, dx):
        return lax.ppermute(t, "rank", [(i, i ^ (dx * cores)) for i in range(n_rank)])

    def to_chip(t, dz, dx):
        if dz == 0:
            return along_x(t, dx)
        if dx == 0:
            return lax.ppermute(t, "node", [(i, i ^ dz) for i in range(n_node)])
        step = dz * n_rank + dx * cores
        return lax.ppermute(t, ("node", "rank"), [(i, i ^ step) for i in range(n_node * n_rank)])

    def swap(t):
        return lax.ppermute(t, "rank", [(i, i ^ 1) for i in range(n_rank)])

    def after(t, *deps):
        return lax.optimization_barrier((t, *deps))[0]

    zs, xs = range(n_node), range(n_x)
    own, mine = prepare(tokens, expert_ids, combine_weights, slot_plan, exp_dev, n_rank)
    near, far, sums, weights = {}, {}, {}, (w_gate, w_up, w_down)

    def run(group, last, pieces=1):
        blocks = sum([near[c] for c in group] + [far[c] for c in group], [])
        keep, *give = ffn(after(mine, *last), blocks, weights, top, weights[0] is w_gate, pieces)
        return keep, give[:pieces], give[pieces:] or weights

    def settle(group, keep, others, wide):
        types = [jnp.float32 if c in wide else jnp.bfloat16 for c in group]
        for c, part in zip(group, join(keep, others, types), strict=True):
            sums[c] = part

    home, across = [(0, 0)], [(0, dx) for dx in xs[1:]]
    column, corner = [(dz, 0) for dz in zs[2:]], [(dz, dx) for dz in zs[2:] for dx in xs[1:]]
    close = [(dz, dx) for dz in zs[1:2] for dx in xs]
    wide = home + [(dz, 0) for dz in zs[1:] if dz != 2]

    near[0, 0] = [own]
    for c in across + close + column:
        near[c] = [to_chip(own, *c)]
    far[0, 0] = [swap(own)]
    keep, give, weights = run(home, [])
    settle(home, keep, [swap(t) for t in give], wide)
    names = across + close + column
    near |= dict(zip(names, after([near[c] for c in names], give), strict=True))

    for dz, _ in reversed(column):
        for dx in xs[1:]:
            near[dz, dx] = [along_x(t, dx) for t in near[dz, 0]]
    for c in names:
        far[c] = [swap(t) for t in near[c]]
    last, waits = give, []
    for group in (column, across + close, corner):
        if not group:
            continue
        if group is corner:
            for c in group:
                near[c] = after(near[c], last)
                far[c] = [swap(t) for t in near[c]]
        keep, last, _ = run(group, last + (waits if group is corner else []))
        settle(group, keep, [swap(t) for t in last], wide)
        if group is column:
            waits = [sums[c] for c in group]

    def send(c):
        more = [along_x(sums[c[0], dx], dx) for dx in xs[1:]] if c[0] not in (0, 2) else []
        return to_chip(add_up([sums[c]] + more, jnp.bfloat16) if more else sums[c], *c)

    early = [(dz, dx) for dz in zs[2:3] for dx in xs] + across
    late = [c for c in across + [(dz, 0) for dz in zs[1:]] if c not in early]
    part = add_up([sums[0, 0]] + [send(c) for c in early], jnp.float32, 10**10) if early else sums[0, 0]
    return add_up([part] + [send(c) for c in late], tokens.dtype)


def power_of_two(n):
    return n & (n - 1) == 0


def local(tokens, expert_ids, combine_weights, slot_plan, w_gate, w_up, w_down):
    n_node, n_rank = lax.axis_size("node"), lax.axis_size("rank")
    tok_rows, top = expert_ids.shape
    exp_dev = w_gate.shape[0]
    slots = n_node * n_rank * exp_dev
    args = (tokens, expert_ids, combine_weights, slot_plan, w_gate, w_up, w_down)
    sent = exp_dev * capacity_of(tok_rows, top, slots)
    fits = 3 * rounded(top) <= LANES and slots <= 256 and power_of_two(n_node) and power_of_two(n_rank) and n_rank > 1
    if fits and 2 * sent > tok_rows:
        return dense(*args, cores=2)
    return routed(*args)


def solution(mesh):
    in_specs = (
        P(("grp", "node", "rank"), None),
        P(("grp", "node", "rank"), None),
        P(("grp", "node", "rank"), None),
        P(),
        P(("node", "rank"), None, None),
        P(("node", "rank"), None, None),
        P(("node", "rank"), None, None),
    )
    out_specs = P(("grp", "node", "rank"), None)
    return jax.shard_map(local, mesh=mesh, in_specs=in_specs, out_specs=out_specs, check_vma=False)
```
